32 devices in a mesh: grp: 2 (over y), wide: 8 (over z, x), narrow: 2 (over core).
Axes of the slice: x: 2, y: 2, z: 4, core: 2. Of those that a mesh axis runs over, the one named last changes fastest.
Arguments:
- activations: bfloat16 [16, 16384], P(('grp', 'narrow'), 'wide'), parts along dimension 0, may hold values from -6 to 6
- w_query: bfloat16 [16384, 8192], P('wide', 'narrow'), may hold values from -0.046875 to 0.046875
- w_keyval: bfloat16 [16384, 4, 2, 128], P('wide', 'narrow'), may hold values from -0.046875 to 0.046875
- cache_keys: bfloat16 [16, 4, 2048, 128], P(('grp', 'wide'), 'narrow'), parts along dimension 0, as said below
- cache_values: bfloat16 [16, 4, 2048, 128], P(('grp', 'wide'), 'narrow'), parts along dimension 0, may hold values from -6 to 6
- lengths: int32 [16], P(('grp', 'wide')), parts along dimension 0, may hold values from 1 to 2048, as said below
- w_out: bfloat16 [8192, 16384], P('narrow', 'wide'), may hold values from -0.5 to 0.5
Outputs:
- attention_out: bfloat16 [16, 16384], P(('grp', 'narrow'), 'wide'), parts along dimension 0
The draws below stay inside these ranges and needn't reach their ends.
There are 2 independent parts, one for each index of `grp`. The reference program is written for one: setup_inputs(seed, part) draws one part's arguments, and reference() takes and returns one part's arrays. A program takes and returns all parts, laid end to end along the dimension named above; an argument that names none is the same for every part. Nothing has to cross between parts.
Inputs may be any that keep to these rules, and one draw needn't show every extreme that they name: `lengths`: each sequence holds 1 to 2048 cached tokens; in every draw some sequence holds exactly 2048. `cache_keys`: cached keys are finite.
All inputs are finite; a program needn't handle non-finite values.
Results may differ from the reference program's by a relative error of at most 0.0076.
Values may be sent and summed in bfloat16 or wider, within the bound.
No kernel may reach another device: no remote copies, remote signals or barrier semaphores. Data moves between devices by JAX's collectives and lax.ppermute only.
A program may use at most 128 MiB of HBM per device.

```python
import math
import jax
import jax.numpy as jnp
from jax import lax

D = 16384
HQ = 64
KVH = 4
HD = 128
CACHE = 2048
SEQS = 8


def draw_cache_keys(key, part):
    key = jax.random.fold_in(key, 11)
    entries = jnp.clip(jax.random.normal(key, (SEQS, KVH, CACHE, HD), jnp.float32), -6.0, 6.0)
    return entries.astype(jnp.bfloat16)


def draw_lengths(key, part):
    key = jax.random.fold_in(key, 23)
    drawn = jax.random.randint(key, (SEQS,), 1, CACHE + 1)
    chosen = jax.random.randint(jax.random.fold_in(key, 5), (), 0, SEQS)
    return jnp.where(jnp.arange(SEQS) == chosen, CACHE, drawn).astype(jnp.int32)


def steps_of(stream_key, dims, shards, smallest, top_value):
    factor_of, own = 1.0, jax.random.fold_in(stream_key, 6)
    for position, parts in shards:
        steps = jnp.exp(jax.random.uniform(jax.random.fold_in(own, position), (parts,), jnp.float32, smallest / len(shards), top_value / len(shards)))
        factor_of = factor_of * jnp.repeat(steps, dims[position] // parts).reshape([-1 if axis == position else 1 for axis in range(len(dims))])
    return factor_of


def scatter_about(rng, extent, spread, most, shards=(), kind=jnp.bfloat16):
    result = jax.random.normal(rng, extent, jnp.float32) * spread
    if len(shards) > 0:
        result = steps_of(rng, extent, shards, -0.22, 0.18) * result
    return jnp.clip(result, min=-most, max=most).astype(kind)


def setup_inputs(seed: int = 0, part: int = 0) -> dict:
    key_list = jax.random.split(jax.random.key(seed), 8)
    own_keys = jax.random.split(jax.random.fold_in(key_list[7], part), 8)
    activations = scatter_about(own_keys[0], (SEQS, D), 1.0, 6.0, ((0, 2), (1, 8)))
    w_query = scatter_about(key_list[1], (D, HQ * HD), D ** -0.5, 0.046875, ((0, 8), (1, 2)))
    w_keyval = scatter_about(key_list[2], (D, KVH, 2, HD), D ** -0.5, 0.046875, ((0, 8), (1, 2)))
    cache_keys = draw_cache_keys(jax.random.fold_in(jax.random.fold_in(key_list[7], part), 71), part)
    cache_values = scatter_about(own_keys[4], (SEQS, KVH, CACHE, HD), 1.0, 6.0, ((0, 8), (1, 2)))
    lengths = draw_lengths(jax.random.fold_in(jax.random.fold_in(key_list[7], part), 71), part)
    w_out = scatter_about(key_list[6], (HQ * HD, D), HD ** -0.5, 0.5, ((0, 2), (1, 8)))
    return dict(activations=activations, w_query=w_query, w_keyval=w_keyval, cache_keys=cache_keys, cache_values=cache_values, lengths=lengths, w_out=w_out)


rope_base = 500000.0

def rotate(values, positions):
    half_width = values.shape[-1] // 2
    frequency = rope_base ** (-jnp.arange(half_width, dtype=jnp.float32) / half_width)
    angles = positions.astype(jnp.float32)[:, None] * frequency[None, :]
    cosine = jnp.cos(angles)[:, None, :]
    sine = jnp.sin(angles)[:, None, :]
    front_half = values[..., :half_width]
    back_half = values[..., half_width:]
    return jnp.concatenate([front_half * cosine - back_half * sine, back_half * cosine + front_half * sine], axis=-1)

def attend(grouped, new_key, new_value, key_rows, value_rows, lengths):
    score_scale = 1.0 / math.sqrt(grouped.shape[-1])
    query_wide = grouped.astype(jnp.float32)
    scores = jnp.einsum('skgd,sktd->skgt', query_wide, key_rows.astype(jnp.float32)) * score_scale
    own_score = jnp.einsum('skgd,skd->skg', query_wide, new_key.astype(jnp.float32)) * score_scale
    slots = jnp.arange(key_rows.shape[2], dtype=jnp.int32)
    visible = slots[None, None, None, :] < lengths.astype(jnp.int32)[:, None, None, None]
    scores = jnp.where(visible, scores, jnp.float32(-1e+30))
    row_max = jnp.maximum(lax.optimization_barrier(jnp.max(scores, axis=-1)), own_score)
    weights = jnp.where(visible, jnp.exp(scores - row_max[..., None]), jnp.float32(0.0))
    own_weight = jnp.exp(own_score - row_max)
    denominator = lax.optimization_barrier(jnp.sum(weights, axis=-1)) + own_weight
    probabilities = (weights / denominator[..., None]).astype(jnp.bfloat16)
    own_prob = (own_weight / denominator).astype(jnp.bfloat16)
    attended = jnp.einsum('skgt,sktd->skgd', probabilities.astype(jnp.float32), value_rows.astype(jnp.float32))
    attended = attended + own_prob.astype(jnp.float32)[..., None] * new_value.astype(jnp.float32)[:, :, None, :]
    return attended.astype(jnp.bfloat16)

def reference(activations, w_query, w_keyval, cache_keys, cache_values, lengths, w_out):
    batch_rows = activations.shape[0]
    queries = jnp.dot(activations, w_query, preferred_element_type=jnp.float32).reshape(batch_rows, HQ, HD)
    key_value = jnp.dot(activations, w_keyval.reshape(D, KVH * 2 * HD), preferred_element_type=jnp.float32)
    key_value = key_value.reshape(batch_rows, KVH, 2, HD)
    rotated = rotate(queries, lengths).astype(jnp.bfloat16).reshape(batch_rows, KVH, HQ // KVH, HD)
    new_key = rotate(key_value[:, :, 0], lengths).astype(jnp.bfloat16)
    new_value = key_value[:, :, 1].astype(jnp.bfloat16)
    attended = attend(rotated, new_key, new_value, cache_keys, cache_values, lengths)
    flat = attended.reshape(batch_rows, HQ * HD)
    return jnp.dot(flat, w_out, preferred_element_type=jnp.float32).astype(jnp.bfloat16)
```

```python
import functools
import math

import jax
import jax.numpy as jnp
from jax import lax
from jax.experimental import pallas as pl
from jax.experimental.pallas import tpu as pltpu
from jax.sharding import PartitionSpec as P

HD = 128
ROPE_BASE = 500000.0
MIB = 2**20
F32, BF16 = jnp.float32, jnp.bfloat16
VMEM = pl.BlockSpec(memory_space=pltpu.VMEM)
SMEM = pl.BlockSpec(memory_space=pltpu.SMEM)
ANY = pl.BlockSpec(memory_space=pl.ANY)


def project_kernel(chunks, core_ref, own_ref, other_ref, w_ref, kv_ref, out_ref, w, kv, sems):
    depth, cols = w_ref.shape
    width = cols // chunks
    kv_copy = pltpu.make_async_copy(kv_ref, kv, sems.at[chunks])
    kv_copy.start()
    copies = []
    for c in range(chunks):
        span = pl.ds(c * width, width)
        copies.append(pltpu.make_async_copy(w_ref.at[:, span], w.at[:, span], sems.at[c]))
        copies[-1].start()

    own, other = own_ref[...].astype(F32), other_ref[...].astype(F32)
    first = core_ref[0] == 0
    wide_rows = jnp.where(
        first, jnp.concatenate([own, other], axis=0), jnp.concatenate([other, own], axis=0)
    )
    rows = wide_rows.astype(BF16)
    count = rows.shape[0]
    heads = cols // HD

    parts = kv_ref.shape[0] // depth
    tiles = depth // HD
    stacked = jnp.concatenate(
        [wide_rows[:, t * HD : (t + 1) * HD] for t in range(tiles)], axis=0
    ).astype(BF16)
    spread_of = lax.broadcasted_iota(jnp.int32, (HD, parts * HD), 0)
    spread_to = lax.broadcasted_iota(jnp.int32, (HD, parts * HD), 1)
    spread = jnp.where(spread_to // parts == spread_of, 1.0, 0.0).astype(BF16)
    repeated = jnp.dot(stacked, spread, preferred_element_type=F32)
    slot = lax.broadcasted_iota(jnp.int32, (count, parts * HD), 1) % parts
    kv_copy.wait()
    total = None
    for t in range(tiles):
        block = repeated[t * count : (t + 1) * count]
        left = jnp.concatenate(
            [jnp.where(slot == p, block, 0.0) for p in range(parts)], axis=0
        ).astype(BF16)
        part = jnp.dot(
            left, kv[t * parts * HD : (t + 1) * parts * HD, :], preferred_element_type=F32
        )
        total = part if total is None else total + part
    for p in range(parts):
        out_ref[:, heads + p, :] = total[p * count : (p + 1) * count]

    for c in range(chunks):
        copies[c].wait()
        block = jnp.dot(rows, w[:, c * width : (c + 1) * width], preferred_element_type=F32)
        for h in range(width // HD):
            out_ref[:, c * (width // HD) + h, :] = block[:, h * HD : (h + 1) * HD]


def attend_kernel(length_ref, cos_ref, sin_ref, parts_ref, keys_ref, values_ref, out_ref):
    summed = parts_ref[0]
    for i in range(1, parts_ref.shape[0]):
        summed = summed + parts_ref[i]
    kv_heads = keys_ref.shape[0]
    heads = parts_ref.shape[1] - 2 * kv_heads
    group = heads // kv_heads
    slots = keys_ref.shape[1]
    rotated = summed * cos_ref[...] + pltpu.roll(summed, HD // 2, 1) * sin_ref[...]
    rotated = rotated.astype(BF16)
    scale = 1.0 / math.sqrt(HD)
    length = length_ref[0]
    visible = lax.broadcasted_iota(jnp.int32, (group, slots), 1) < length
    attended = []
    for k in range(kv_heads):
        query = rotated[k * group : (k + 1) * group]
        new_key = rotated[heads + 2 * k : heads + 2 * k + 1].astype(F32)
        new_value = summed[heads + 2 * k + 1 : heads + 2 * k + 2].astype(BF16).astype(F32)
        scores = (
            lax.dot_general(
                query, keys_ref[k], (((1,), (1,)), ((), ())), preferred_element_type=F32
            )
            * scale
        )
        own = jnp.sum(query.astype(F32) * new_key, axis=-1, keepdims=True) * scale
        scores = jnp.where(visible, scores, -1e30)
        top = jnp.maximum(jnp.max(scores, axis=-1, keepdims=True), own)
        weights = jnp.where(visible, jnp.exp(scores - top), 0.0)
        own_weight = jnp.exp(own - top)
        denominator = jnp.sum(weights, axis=-1, keepdims=True) + own_weight
        probabilities = (weights / denominator).astype(BF16)
        own_prob = (own_weight / denominator).astype(BF16).astype(F32)
        result = jnp.dot(probabilities, values_ref[k], preferred_element_type=F32)
        attended.append((result + own_prob * new_value).astype(BF16))
    block = jnp.concatenate(attended, axis=0)
    for i in range(out_ref.shape[0]):
        out_ref[i] = block


def output_kernel(core_ref, flat_ref, w_ref, keep_ref, send_ref):
    depth, cols = w_ref.shape
    count = keep_ref.shape[0] * 2
    heads = depth // HD
    size = 8 * heads
    to = lax.broadcasted_iota(jnp.int32, (size, size), 0)
    come = lax.broadcasted_iota(jnp.int32, (size, size), 1)
    order = jnp.where((to % 8) * heads + to // 8 == come, 1.0, 0.0).astype(BF16)
    groups = [
        jnp.dot(order, flat_ref[g * size : (g + 1) * size, :], preferred_element_type=F32)
        for g in range(count // 8)
    ]
    left = jnp.concatenate(
        [
            jnp.concatenate([part[h * 8 : (h + 1) * 8] for part in groups], axis=0)
            for h in range(heads)
        ],
        axis=1,
    ).astype(BF16)
    half = count // 2
    first = core_ref[0] == 0
    width = 256
    for c in range(cols // width):
        span = slice(c * width, (c + 1) * width)
        part = jnp.dot(left, w_ref[:, span], preferred_element_type=F32)
        low, high = part[:half, :], part[half:, :]
        keep_ref[:, span] = jnp.where(first, low, high)
        send_ref[:, span] = jnp.where(first, high, low)


def local(activations, w_query, w_keyval, cache_keys, cache_values, lengths, w_out):
    receivers = lax.axis_size("wide")
    core = lax.axis_index("narrow").astype(jnp.int32).reshape(1)
    swap = [(0, 1), (1, 0)]
    rows = activations.shape[0] * 2
    depth, cols = w_query.shape
    kv_heads = w_keyval.shape[1]
    heads = cols // HD
    out_cols = w_out.shape[1]
    half_width = HD // 2

    frequency = ROPE_BASE ** (-jnp.arange(half_width, dtype=F32) / half_width)
    angles = lengths.astype(F32)[:, None] * frequency[None, :]
    cosine, sine = jnp.cos(angles), jnp.sin(angles)
    cosine = jnp.concatenate([cosine, cosine], axis=-1)
    sine = jnp.concatenate([-sine, sine], axis=-1)

    other = lax.ppermute(activations, "narrow", swap)
    q_chunks = 8
    kv_rows = w_keyval.reshape(depth * kv_heads * 2, HD)
    partial = pl.pallas_call(
        functools.partial(project_kernel, q_chunks),
        out_shape=jax.ShapeDtypeStruct((rows, heads + 2 * kv_heads, HD), F32),
        in_specs=[SMEM, VMEM, VMEM, ANY, ANY],
        out_specs=VMEM,
        scratch_shapes=[
            pltpu.VMEM((depth, cols), BF16),
            pltpu.VMEM(kv_rows.shape, BF16),
            pltpu.SemaphoreType.DMA((q_chunks + 1,)),
        ],
        compiler_params=pltpu.CompilerParams(vmem_limit_bytes=46 * MIB),
        cost_estimate=pl.CostEstimate(
            flops=2 * rows * depth * cols, bytes_accessed=18 * MIB, transcendentals=0
        ),
    )(core, activations, other, w_query, kv_rows)
    parts = lax.all_to_all(partial, "wide", 0, 0, tiled=True)
    attended = pl.pallas_call(
        attend_kernel,
        out_shape=jax.ShapeDtypeStruct((receivers, heads, HD), BF16),
        in_specs=[SMEM, VMEM, VMEM, VMEM, VMEM, VMEM],
        out_specs=VMEM,
        compiler_params=pltpu.CompilerParams(vmem_limit_bytes=8 * MIB),
        cost_estimate=pl.CostEstimate(
            flops=4 * heads * 2048 * HD, bytes_accessed=2 * MIB, transcendentals=heads * 2048
        ),
    )(lengths, cosine, sine, parts, cache_keys[0], cache_values[0])
    gathered = lax.all_to_all(attended, "wide", 0, 0, tiled=True)
    keep, send = pl.pallas_call(
        output_kernel,
        out_shape=[jax.ShapeDtypeStruct((rows // 2, out_cols), F32)] * 2,
        in_specs=[SMEM, VMEM, VMEM],
        out_specs=[VMEM, VMEM],
        compiler_params=pltpu.CompilerParams(vmem_limit_bytes=20 * MIB),
        cost_estimate=pl.CostEstimate(
            flops=2 * rows * heads * HD * out_cols, bytes_accessed=16 * MIB, transcendentals=0
        ),
    )(core, gathered.reshape(rows * heads, HD), w_out)
    return (keep + lax.ppermute(send, "narrow", swap)).astype(BF16)


def solution(mesh):
    placed = (
        P(("grp", "narrow"), "wide"),
        P("wide", "narrow"),
        P("wide", "narrow", None, None),
        P(("grp", "wide"), "narrow", None, None),
        P(("grp", "wide"), "narrow", None, None),
        P(("grp", "wide")),
        P("narrow", "wide"),
    )
    return jax.shard_map(
        local, mesh=mesh, in_specs=placed, out_specs=P(("grp", "narrow"), "wide"), check_vma=False
    )
```

```python
import functools
import math

import jax
import jax.numpy as jnp
from jax import lax
from jax.experimental import pallas as pl
from jax.experimental.pallas import tpu as pltpu
from jax.sharding import PartitionSpec as P

HD = 128
ROPE_BASE = 500000.0
MIB = 2**20
F32, BF16 = jnp.float32, jnp.bfloat16
VMEM = pl.BlockSpec(memory_space=pltpu.VMEM)
SMEM = pl.BlockSpec(memory_space=pltpu.SMEM)
ANY = pl.BlockSpec(memory_space=pl.ANY)


def in_hbm(array):
    return pltpu.with_memory_space_constraint(array, pltpu.HBM)


def in_vmem(array):
    return pltpu.with_memory_space_constraint(array, pltpu.VMEM)


def project_kernel(chunks, core_ref, after_ref, own_hbm, other_ref, w_ref, kv_ref, out_ref, own_ref, w, kv, sems):
    depth, cols = w_ref.shape
    width = cols // chunks
    own_copy = pltpu.make_async_copy(own_hbm, own_ref, sems.at[chunks + 1])
    own_copy.start()
    kv_copy = pltpu.make_async_copy(kv_ref, kv, sems.at[chunks])
    kv_copy.start()
    copies = []
    for c in range(chunks):
        span = pl.ds(c * width, width)
        copies.append(pltpu.make_async_copy(w_ref.at[:, span], w.at[:, span], sems.at[c]))
        copies[-1].start()

    own_copy.wait()
    own, other = own_ref[...].astype(F32), other_ref[...].astype(F32)
    first = core_ref[0] == 0
    wide_rows = jnp.where(
        first, jnp.concatenate([own, other], axis=0), jnp.concatenate([other, own], axis=0)
    )
    rows = wide_rows.astype(BF16)
    count = rows.shape[0]
    heads = cols // HD

    parts = kv_ref.shape[0] // depth
    tiles = depth // HD
    stacked = jnp.concatenate(
        [wide_rows[:, t * HD : (t + 1) * HD] for t in range(tiles)], axis=0
    ).astype(BF16)
    spread_of = lax.broadcasted_iota(jnp.int32, (HD, parts * HD), 0)
    spread_to = lax.broadcasted_iota(jnp.int32, (HD, parts * HD), 1)
    spread = jnp.where(spread_to // parts == spread_of, 1.0, 0.0).astype(BF16)
    repeated = jnp.dot(stacked, spread, preferred_element_type=F32)
    slot = lax.broadcasted_iota(jnp.int32, (count, parts * HD), 1) % parts
    kv_copy.wait()
    total = None
    for t in range(tiles):
        block = repeated[t * count : (t + 1) * count]
        left = jnp.concatenate(
            [jnp.where(slot == p, block, 0.0) for p in range(parts)], axis=0
        ).astype(BF16)
        part = jnp.dot(
            left, kv[t * parts * HD : (t + 1) * parts * HD, :], preferred_element_type=F32
        )
        total = part if total is None else total + part
    for p in range(parts):
        out_ref[:, heads + p, :] = total[p * count : (p + 1) * count]

    for c in range(chunks):
        copies[c].wait()
        block = jnp.dot(rows, w[:, c * width : (c + 1) * width], preferred_element_type=F32)
        for h in range(width // HD):
            out_ref[:, c * (width // HD) + h, :] = block[:, h * HD : (h + 1) * HD]


def attend_kernel(length_ref, turns_ref, parts_ref, keys_ref, values_ref, out_ref):
    summed = parts_ref[0]
    for i in range(1, parts_ref.shape[0]):
        summed = summed + parts_ref[i]
    kv_heads = keys_ref.shape[0]
    heads = parts_ref.shape[1] - 2 * kv_heads
    group = heads // kv_heads
    slots = keys_ref.shape[1]
    rotated = summed * turns_ref[:1] + pltpu.roll(summed, HD // 2, 1) * turns_ref[1:]
    rotated = rotated.astype(BF16)
    scale = 1.0 / math.sqrt(HD)
    length = length_ref[0]
    visible = lax.broadcasted_iota(jnp.int32, (group, slots), 1) < length
    attended = []
    for k in range(kv_heads):
        query = rotated[k * group : (k + 1) * group]
        new_key = rotated[heads + 2 * k : heads + 2 * k + 1].astype(F32)
        new_value = summed[heads + 2 * k + 1 : heads + 2 * k + 2].astype(BF16).astype(F32)
        scores = (
            lax.dot_general(
                query, keys_ref[k], (((1,), (1,)), ((), ())), preferred_element_type=F32
            )
            * scale
        )
        own = jnp.sum(query.astype(F32) * new_key, axis=-1, keepdims=True) * scale
        scores = jnp.where(visible, scores, -1e30)
        top = jnp.maximum(jnp.max(scores, axis=-1, keepdims=True), own)
        weights = jnp.where(visible, jnp.exp(scores - top), 0.0)
        own_weight = jnp.exp(own - top)
        denominator = jnp.sum(weights, axis=-1, keepdims=True) + own_weight
        probabilities = (weights / denominator).astype(BF16)
        own_prob = (own_weight / denominator).astype(BF16).astype(F32)
        result = jnp.dot(probabilities, values_ref[k], preferred_element_type=F32)
        attended.append((result + own_prob * new_value).astype(BF16))
    block = jnp.concatenate(attended, axis=0)
    for i in range(out_ref.shape[0]):
        out_ref[i] = block


def output_kernel(core_ref, flat_ref, w_ref, keep_ref, send_ref):
    depth, cols = w_ref.shape
    count = keep_ref.shape[0] * 2
    heads = depth // HD
    size = 8 * heads
    to = lax.broadcasted_iota(jnp.int32, (size, size), 0)
    come = lax.broadcasted_iota(jnp.int32, (size, size), 1)
    order = jnp.where((to % 8) * heads + to // 8 == come, 1.0, 0.0).astype(BF16)
    groups = [
        jnp.dot(order, flat_ref[g * size : (g + 1) * size, :], preferred_element_type=F32)
        for g in range(count // 8)
    ]
    left = jnp.concatenate(
        [
            jnp.concatenate([part[h * 8 : (h + 1) * 8] for part in groups], axis=0)
            for h in range(heads)
        ],
        axis=1,
    ).astype(BF16)
    half = count // 2
    first = core_ref[0] == 0
    width = 256
    for c in range(cols // width):
        span = slice(c * width, (c + 1) * width)
        part = jnp.dot(left, w_ref[:, span], preferred_element_type=F32)
        low, high = part[:half, :], part[half:, :]
        keep_ref[:, span] = jnp.where(first, low, high)
        send_ref[:, span] = jnp.where(first, high, low)


def local(activations, w_query, w_keyval, cache_keys, cache_values, lengths, w_out):
    receivers = lax.axis_size("wide")
    core = lax.axis_index("narrow").astype(jnp.int32).reshape(1)
    swap = [(0, 1), (1, 0)]
    rows = activations.shape[0] * 2
    depth, cols = w_query.shape
    kv_heads = w_keyval.shape[1]
    heads = cols // HD
    out_cols = w_out.shape[1]
    half_width = HD // 2

    frequency = ROPE_BASE ** (-jnp.arange(half_width, dtype=F32) / half_width)
    angles = lengths.astype(F32)[:, None] * frequency[None, :]
    cosine, sine = jnp.cos(angles), jnp.sin(angles)
    turns = jnp.concatenate([cosine, cosine, -sine, sine], axis=-1).reshape(2, HD)

    other = lax.ppermute(activations, "narrow", swap)
    q_chunks = 8
    kv_rows = w_keyval.reshape(depth * kv_heads * 2, HD)
    partial = pl.pallas_call(
        functools.partial(project_kernel, q_chunks),
        out_shape=pltpu.VMEM((rows, heads + 2 * kv_heads, HD), F32),
        in_specs=[SMEM, ANY, ANY, VMEM, ANY, ANY],
        out_specs=VMEM,
        scratch_shapes=[
            pltpu.VMEM(activations.shape, BF16),
            pltpu.VMEM((depth, cols), BF16),
            pltpu.VMEM(kv_rows.shape, BF16),
            pltpu.SemaphoreType.DMA((q_chunks + 2,)),
        ],
        compiler_params=pltpu.CompilerParams(vmem_limit_bytes=24 * MIB),
        cost_estimate=pl.CostEstimate(
            flops=2 * rows * depth * cols, bytes_accessed=18 * MIB, transcendentals=0
        ),
    )(core, turns, in_hbm(activations), other, in_hbm(w_query), in_hbm(kv_rows))
    parts = lax.all_to_all(partial, "wide", 0, 0, tiled=True)
    attended = pl.pallas_call(
        attend_kernel,
        out_shape=jax.ShapeDtypeStruct((receivers, heads, HD), BF16),
        in_specs=[SMEM, VMEM, VMEM, VMEM, VMEM],
        out_specs=VMEM,
        compiler_params=pltpu.CompilerParams(vmem_limit_bytes=8 * MIB),
        cost_estimate=pl.CostEstimate(
            flops=4 * heads * 2048 * HD, bytes_accessed=2 * MIB, transcendentals=heads * 2048
        ),
    )(lengths, turns, parts, cache_keys[0], cache_values[0])
    gathered = lax.all_to_all(attended, "wide", 0, 0, tiled=True)
    keep, send = pl.pallas_call(
        output_kernel,
        out_shape=[jax.ShapeDtypeStruct((rows // 2, out_cols), F32)] * 2,
        in_specs=[SMEM, VMEM, VMEM],
        out_specs=[VMEM, VMEM],
        compiler_params=pltpu.CompilerParams(vmem_limit_bytes=20 * MIB),
        cost_estimate=pl.CostEstimate(
            flops=2 * rows * heads * HD * out_cols, bytes_accessed=16 * MIB, transcendentals=0
        ),
    )(core, gathered.reshape(rows * heads, HD), in_vmem(w_out))
    return (keep + lax.ppermute(send, "narrow", swap)).astype(BF16)


def solution(mesh):
    placed = (
        P(("grp", "narrow"), "wide"),
        P("wide", "narrow"),
        P("wide", "narrow", None, None),
        P(("grp", "wide"), "narrow", None, None),
        P(("grp", "wide"), "narrow", None, None),
        P(("grp", "wide")),
        P("narrow", "wide"),
    )
    return jax.shard_map(
        local, mesh=mesh, in_specs=placed, out_specs=P(("grp", "narrow"), "wide"), check_vma=False
    )
```

```python
import functools
import math

import jax
import jax.numpy as jnp
from jax import lax
from jax.experimental import pallas as pl
from jax.experimental.pallas import tpu as pltpu
from jax.sharding import PartitionSpec as P

HD = 128
ROPE_BASE = 500000.0
MIB = 2**20
F32, BF16 = jnp.float32, jnp.bfloat16
SPAN = 7_000_000_000
VMEM = pl.BlockSpec(memory_space=pltpu.VMEM)
SMEM = pl.BlockSpec(memory_space=pltpu.SMEM)
ANY = pl.BlockSpec(memory_space=pl.ANY)


def in_hbm(array):
    return pltpu.with_memory_space_constraint(array, pltpu.HBM)


def in_vmem(array):
    return pltpu.with_memory_space_constraint(array, pltpu.VMEM)


def turns_kernel(cosine_ref, sine_ref, out_ref):
    cosine, sine = cosine_ref[...], sine_ref[...]
    out_ref[...] = jnp.concatenate(
        [jnp.concatenate([cosine, cosine], axis=1), jnp.concatenate([-sine, sine], axis=1)], axis=0
    )


def project_kernel(
    heights, core_ref, after_ref, own_hbm, other_ref, w_ref, kv_ref, sums, own_ref, w, held, sems
):
    depth, cols = w_ref.shape
    own_copy = pltpu.make_async_copy(own_hbm, own_ref, sems.at[len(heights)])
    own_copy.start()
    copies, spans, at = [], [], 0
    for c, height in enumerate(heights):
        span = pl.ds(at, height)
        copies.append(pltpu.make_async_copy(w_ref.at[span], w.at[span], sems.at[c]))
        copies[-1].start()
        spans.append((at, height))
        at += height

    own_copy.wait()
    own, other = own_ref[...].astype(F32), other_ref[...].astype(F32)
    first = core_ref[0] == 0
    wide_rows = jnp.where(
        first, jnp.concatenate([own, other], axis=0), jnp.concatenate([other, own], axis=0)
    )
    rows = wide_rows.astype(BF16)
    count = rows.shape[0]
    heads = cols // HD

    parts = kv_ref.shape[0] // depth
    tiles = depth // HD
    stacked = jnp.concatenate(
        [wide_rows[:, t * HD : (t + 1) * HD] for t in range(tiles)], axis=0
    ).astype(BF16)
    spread_of = lax.broadcasted_iota(jnp.int32, (HD, parts * HD), 0)
    spread_to = lax.broadcasted_iota(jnp.int32, (HD, parts * HD), 1)
    spread = jnp.where(spread_to // parts == spread_of, 1.0, 0.0).astype(BF16)
    repeated = jnp.dot(stacked, spread, preferred_element_type=F32)
    slot = lax.broadcasted_iota(jnp.int32, (count, parts * HD), 1) % parts
    total = None
    for t in range(tiles):
        block = repeated[t * count : (t + 1) * count]
        left = jnp.concatenate(
            [jnp.where(slot == p, block, 0.0) for p in range(parts)], axis=0
        ).astype(BF16)
        part = jnp.dot(
            left, kv_ref[t * parts * HD : (t + 1) * parts * HD, :], preferred_element_type=F32
        )
        total = part if total is None else total + part
    for p in range(parts):
        sums[:, heads + p, :] = total[p * count : (p + 1) * count]

    for c, (at, height) in enumerate(spans):
        copies[c].wait()
        block = jnp.dot(
            rows[:, at : at + height], w[at : at + height, :], preferred_element_type=F32
        )
        if c > 0:
            block = block + held[...]
        if c < len(spans) - 1:
            held[...] = block
    for h in range(heads):
        sums[:, h, :] = block[:, h * HD : (h + 1) * HD]


def attend_kernel(length_ref, turns_ref, parts_ref, keys_ref, values_ref, out_ref):
    summed = parts_ref[0]
    for i in range(1, parts_ref.shape[0]):
        summed = summed + parts_ref[i]
    kv_heads = keys_ref.shape[0]
    heads = parts_ref.shape[1] - 2 * kv_heads
    group = heads // kv_heads
    slots = keys_ref.shape[1]
    rotated = summed * turns_ref[:1] + pltpu.roll(summed, HD // 2, 1) * turns_ref[1:]
    rotated = rotated.astype(BF16)
    scale = 1.0 / math.sqrt(HD)
    length = length_ref[0]
    visible = lax.broadcasted_iota(jnp.int32, (group, slots), 1) < length
    attended = []
    for k in range(kv_heads):
        query = rotated[k * group : (k + 1) * group]
        new_key = rotated[heads + 2 * k : heads + 2 * k + 1].astype(F32)
        new_value = summed[heads + 2 * k + 1 : heads + 2 * k + 2].astype(BF16).astype(F32)
        scores = (
            lax.dot_general(
                query, keys_ref[k], (((1,), (1,)), ((), ())), preferred_element_type=F32
            )
            * scale
        )
        own = jnp.sum(query.astype(F32) * new_key, axis=-1, keepdims=True) * scale
        scores = jnp.where(visible, scores, -1e30)
        top = jnp.maximum(jnp.max(scores, axis=-1, keepdims=True), own)
        weights = jnp.where(visible, jnp.exp(scores - top), 0.0)
        own_weight = jnp.exp(own - top)
        denominator = jnp.sum(weights, axis=-1, keepdims=True) + own_weight
        inverse = 1.0 / denominator
        probabilities = (weights * inverse).astype(BF16)
        own_prob = (own_weight * inverse).astype(BF16).astype(F32)
        result = jnp.dot(probabilities, values_ref[k], preferred_element_type=F32)
        attended.append((result + own_prob * new_value).astype(BF16))
    block = jnp.concatenate(attended, axis=0)
    for i in range(out_ref.shape[0]):
        out_ref[i] = block


def output_kernel(core_ref, flat_ref, w_ref, keep_ref, send_ref):
    depth, cols = w_ref.shape
    count = keep_ref.shape[0] * 2
    heads = depth // HD
    size = 8 * heads
    to = lax.broadcasted_iota(jnp.int32, (size, size), 0)
    come = lax.broadcasted_iota(jnp.int32, (size, size), 1)
    order = jnp.where((to % 8) * heads + to // 8 == come, 1.0, 0.0).astype(BF16)
    groups = [
        jnp.dot(order, flat_ref[g * size : (g + 1) * size, :], preferred_element_type=F32)
        for g in range(count // 8)
    ]
    left = jnp.concatenate(
        [
            jnp.concatenate([part[h * 8 : (h + 1) * 8] for part in groups], axis=0)
            for h in range(heads)
        ],
        axis=1,
    ).astype(BF16)
    half = count // 2
    first = core_ref[0] == 0
    width = 1024
    for c in range(cols // width):
        span = slice(c * width, (c + 1) * width)
        part = jnp.dot(left, w_ref[:, span], preferred_element_type=F32)
        low, high = part[:half, :], part[half:, :]
        keep_ref[:, span] = jnp.where(first, low, high)
        send_ref[:, span] = jnp.where(first, high, low)


def local(activations, w_query, w_keyval, cache_keys, cache_values, lengths, w_out):
    receivers = lax.axis_size("wide")
    core = lax.axis_index("narrow").astype(jnp.int32).reshape(1)
    swap = [(0, 1), (1, 0)]
    rows = activations.shape[0] * 2
    depth, cols = w_query.shape
    kv_heads = w_keyval.shape[1]
    heads = cols // HD
    out_cols = w_out.shape[1]
    half_width = HD // 2

    frequency = ROPE_BASE ** (-jnp.arange(half_width, dtype=F32) / half_width)
    angles = lengths.astype(F32)[:, None] * frequency[None, :]
    cosine, sine = jnp.cos(angles), jnp.sin(angles)
    turns = pl.pallas_call(
        turns_kernel,
        out_shape=jax.ShapeDtypeStruct((2, HD), F32),
        in_specs=[VMEM, VMEM],
        out_specs=VMEM,
        compiler_params=pltpu.CompilerParams(vmem_limit_bytes=MIB),
        cost_estimate=pl.CostEstimate(flops=SPAN, bytes_accessed=MIB, transcendentals=0),
    )(cosine, sine)

    other = lax.ppermute(activations, "narrow", swap)
    heights = [depth // 8] * 7 + [depth // 16] * 2 if depth % 256 == 0 else [depth]
    kv_rows = w_keyval.reshape(depth * kv_heads * 2, HD)
    partial = pl.pallas_call(
        functools.partial(project_kernel, heights),
        out_shape=pltpu.VMEM((rows, heads + 2 * kv_heads, HD), F32),
        in_specs=[SMEM, ANY, ANY, VMEM, ANY, VMEM],
        out_specs=VMEM,
        scratch_shapes=[
            pltpu.VMEM(activations.shape, BF16),
            pltpu.VMEM((depth, cols), BF16),
            pltpu.VMEM((rows, cols), F32),
            pltpu.SemaphoreType.DMA((len(heights) + 1,)),
        ],
        compiler_params=pltpu.CompilerParams(vmem_limit_bytes=24 * MIB),
        cost_estimate=pl.CostEstimate(
            flops=SPAN, bytes_accessed=18 * MIB, transcendentals=0
        ),
    )(core, turns, in_hbm(activations), other, in_hbm(w_query), in_vmem(kv_rows))
    parts = lax.all_to_all(partial, "wide", 0, 0, tiled=True)
    attended = pl.pallas_call(
        attend_kernel,
        out_shape=jax.ShapeDtypeStruct((receivers, heads, HD), BF16),
        in_specs=[SMEM, VMEM, VMEM, VMEM, VMEM],
        out_specs=VMEM,
        compiler_params=pltpu.CompilerParams(vmem_limit_bytes=8 * MIB),
        cost_estimate=pl.CostEstimate(
            flops=SPAN, bytes_accessed=2 * MIB, transcendentals=heads * 2048
        ),
    )(lengths, turns, parts, cache_keys[0], cache_values[0])
    gathered = lax.all_to_all(attended, "wide", 0, 0, tiled=True)
    keep, send = pl.pallas_call(
        output_kernel,
        out_shape=[jax.ShapeDtypeStruct((rows // 2, out_cols), F32)] * 2,
        in_specs=[SMEM, VMEM, VMEM],
        out_specs=[VMEM, VMEM],
        compiler_params=pltpu.CompilerParams(vmem_limit_bytes=20 * MIB),
        cost_estimate=pl.CostEstimate(
            flops=2 * rows * heads * HD * out_cols, bytes_accessed=16 * MIB, transcendentals=0
        ),
    )(core, gathered.reshape(rows * heads, HD), in_vmem(w_out))
    return (keep + lax.ppermute(send, "narrow", swap)).astype(BF16)


def solution(mesh):
    placed = (
        P(("grp", "narrow"), "wide"),
        P("wide", "narrow"),
        P("wide", "narrow", None, None),
        P(("grp", "wide"), "narrow", None, None),
        P(("grp", "wide"), "narrow", None, None),
        P(("grp", "wide")),
        P("narrow", "wide"),
    )
    return jax.shard_map(
        local, mesh=mesh, in_specs=placed, out_specs=P(("grp", "narrow"), "wide"), check_vma=False
    )
```

```python
import functools
import math

import jax
import jax.numpy as jnp
from jax import lax
from jax.experimental import pallas as pl
from jax.experimental.pallas import tpu as pltpu
from jax.sharding import PartitionSpec as P

HD = 128
ROPE_BASE = 500000.0
MIB = 2**20
F32, BF16 = jnp.float32, jnp.bfloat16
SPAN = 7_000_000_000
VMEM = pl.BlockSpec(memory_space=pltpu.VMEM)
SMEM = pl.BlockSpec(memory_space=pltpu.SMEM)
ANY = pl.BlockSpec(memory_space=pl.ANY)


def in_hbm(array):
    return pltpu.with_memory_space_constraint(array, pltpu.HBM)


def in_vmem(array):
    return pltpu.with_memory_space_constraint(array, pltpu.VMEM)


def turns_kernel(cosine_ref, sine_ref, out_ref):
    cosine, sine = cosine_ref[...], sine_ref[...]
    out_ref[...] = jnp.concatenate(
        [jnp.concatenate([cosine, cosine], axis=1), jnp.concatenate([-sine, sine], axis=1)], axis=0
    )


def project_kernel(
    heights, core_ref, after_ref, own_hbm, other_ref, w_ref, kv_ref, sums, own_ref, w, held, sems
):
    depth, cols = w_ref.shape
    own_copy = pltpu.make_async_copy(own_hbm, own_ref, sems.at[len(heights)])
    own_copy.start()
    copies, spans, at = [], [], 0
    for c, height in enumerate(heights):
        span = pl.ds(at, height)
        copies.append(pltpu.make_async_copy(w_ref.at[span], w.at[span], sems.at[c]))
        copies[-1].start()
        spans.append((at, height))
        at += height

    own_copy.wait()
    own, other = own_ref[...].astype(F32), other_ref[...].astype(F32)
    first = core_ref[0] == 0
    wide_rows = jnp.where(
        first, jnp.concatenate([own, other], axis=0), jnp.concatenate([other, own], axis=0)
    )
    rows = wide_rows.astype(BF16)
    count = rows.shape[0]
    heads = cols // HD

    parts = kv_ref.shape[0] // depth
    tiles = depth // HD
    stacked = jnp.concatenate(
        [wide_rows[:, t * HD : (t + 1) * HD] for t in range(tiles)], axis=0
    ).astype(BF16)
    spread_of = lax.broadcasted_iota(jnp.int32, (HD, parts * HD), 0)
    spread_to = lax.broadcasted_iota(jnp.int32, (HD, parts * HD), 1)
    spread = jnp.where(spread_to // parts == spread_of, 1.0, 0.0).astype(BF16)
    repeated = jnp.dot(stacked, spread, preferred_element_type=F32)
    slot = lax.broadcasted_iota(jnp.int32, (count, parts * HD), 1) % parts
    total = None
    for t in range(tiles):
        block = repeated[t * count : (t + 1) * count]
        left = jnp.concatenate(
            [jnp.where(slot == p, block, 0.0) for p in range(parts)], axis=0
        ).astype(BF16)
        part = jnp.dot(
            left, kv_ref[t * parts * HD : (t + 1) * parts * HD, :], preferred_element_type=F32
        )
        total = part if total is None else total + part
    for p in range(parts):
        sums[:, heads + p, :] = total[p * count : (p + 1) * count]

    for c, (at, height) in enumerate(spans):
        copies[c].wait()
        block = jnp.dot(
            rows[:, at : at + height], w[at : at + height, :], preferred_element_type=F32
        )
        if c > 0:
            block = block + held[...]
        if c < len(spans) - 1:
            held[...] = block
    for h in range(heads):
        sums[:, h, :] = block[:, h * HD : (h + 1) * HD]


def attend_kernel(length_ref, turns_ref, parts_ref, keys_ref, values_ref, out_ref):
    summed = parts_ref[0]
    for i in range(1, parts_ref.shape[0]):
        summed = summed + parts_ref[i]
    kv_heads = keys_ref.shape[0]
    heads = parts_ref.shape[1] - 2 * kv_heads
    group = heads // kv_heads
    slots = keys_ref.shape[1]
    rotated = summed * turns_ref[:1] + pltpu.roll(summed, HD // 2, 1) * turns_ref[1:]
    rotated = rotated.astype(BF16)
    scale = 1.0 / math.sqrt(HD)
    length = length_ref[0]
    visible = lax.broadcasted_iota(jnp.int32, (heads, slots), 1) < length
    groups = [slice(k * group, (k + 1) * group) for k in range(kv_heads)]
    scores = [
        lax.dot_general(
            rotated[rows], keys_ref[k], (((1,), (1,)), ((), ())), preferred_element_type=F32
        )
        for k, rows in enumerate(groups)
    ]
    scores = jnp.concatenate(scores, axis=0) * scale
    new_key, new_value = [], []
    for k in range(kv_heads):
        at = heads + 2 * k
        new_key.append(jnp.broadcast_to(rotated[at : at + 1].astype(F32), (group, HD)))
        value = summed[at + 1 : at + 2].astype(BF16).astype(F32)
        new_value.append(jnp.broadcast_to(value, (group, HD)))
    new_key, new_value = jnp.concatenate(new_key, axis=0), jnp.concatenate(new_value, axis=0)
    own = jnp.sum(rotated[:heads].astype(F32) * new_key, axis=-1, keepdims=True) * scale
    scores = jnp.where(visible, scores, -1e30)
    top = jnp.maximum(jnp.max(scores, axis=-1, keepdims=True), own)
    weights = jnp.where(visible, jnp.exp(scores - top), 0.0)
    own_weight = jnp.exp(own - top)
    inverse = 1.0 / (jnp.sum(weights, axis=-1, keepdims=True) + own_weight)
    probabilities = (weights * inverse).astype(BF16)
    own_prob = (own_weight * inverse).astype(BF16).astype(F32)
    result = [
        jnp.dot(probabilities[rows], values_ref[k], preferred_element_type=F32)
        for k, rows in enumerate(groups)
    ]
    block = (jnp.concatenate(result, axis=0) + own_prob * new_value).astype(BF16)
    for i in range(out_ref.shape[0]):
        out_ref[i] = block


def output_kernel(core_ref, flat_ref, w_ref, keep_ref, send_ref):
    depth, cols = w_ref.shape
    count = keep_ref.shape[0] * 2
    heads = depth // HD
    size = 8 * heads
    to = lax.broadcasted_iota(jnp.int32, (size, size), 0)
    come = lax.broadcasted_iota(jnp.int32, (size, size), 1)
    order = jnp.where((to % 8) * heads + to // 8 == come, 1.0, 0.0).astype(BF16)
    groups = [
        jnp.dot(order, flat_ref[g * size : (g + 1) * size, :], preferred_element_type=F32)
        for g in range(count // 8)
    ]
    left = jnp.concatenate(
        [
            jnp.concatenate([part[h * 8 : (h + 1) * 8] for part in groups], axis=0)
            for h in range(heads)
        ],
        axis=1,
    ).astype(BF16)
    half = count // 2
    first = core_ref[0] == 0
    width = 1024
    for c in range(cols // width):
        span = slice(c * width, (c + 1) * width)
        part = jnp.dot(left, w_ref[:, span], preferred_element_type=F32)
        low, high = part[:half, :], part[half:, :]
        keep_ref[:, span] = jnp.where(first, low, high)
        send_ref[:, span] = jnp.where(first, high, low)


def local(activations, w_query, w_keyval, cache_keys, cache_values, lengths, w_out):
    receivers = lax.axis_size("wide")
    core = lax.axis_index("narrow").astype(jnp.int32).reshape(1)
    swap = [(0, 1), (1, 0)]
    rows = activations.shape[0] * 2
    depth, cols = w_query.shape
    kv_heads = w_keyval.shape[1]
    heads = cols // HD
    out_cols = w_out.shape[1]
    half_width = HD // 2

    frequency = ROPE_BASE ** (-jnp.arange(half_width, dtype=F32) / half_width)
    angles = lengths.astype(F32)[:, None] * frequency[None, :]
    cosine, sine = jnp.cos(angles), jnp.sin(angles)
    turns = pl.pallas_call(
        turns_kernel,
        out_shape=jax.ShapeDtypeStruct((2, HD), F32),
        in_specs=[VMEM, VMEM],
        out_specs=VMEM,
        compiler_params=pltpu.CompilerParams(vmem_limit_bytes=MIB),
        cost_estimate=pl.CostEstimate(flops=SPAN, bytes_accessed=MIB, transcendentals=0),
    )(cosine, sine)

    other = lax.ppermute(activations, "narrow", swap)
    heights = [depth // 8] * 7 + [depth // 16] * 2 if depth % 256 == 0 else [depth]
    kv_rows = w_keyval.reshape(depth * kv_heads * 2, HD)
    partial = pl.pallas_call(
        functools.partial(project_kernel, heights),
        out_shape=pltpu.VMEM((rows, heads + 2 * kv_heads, HD), F32),
        in_specs=[SMEM, ANY, ANY, VMEM, ANY, VMEM],
        out_specs=VMEM,
        scratch_shapes=[
            pltpu.VMEM(activations.shape, BF16),
            pltpu.VMEM((depth, cols), BF16),
            pltpu.VMEM((rows, cols), F32),
            pltpu.SemaphoreType.DMA((len(heights) + 1,)),
        ],
        compiler_params=pltpu.CompilerParams(vmem_limit_bytes=24 * MIB),
        cost_estimate=pl.CostEstimate(
            flops=SPAN, bytes_accessed=18 * MIB, transcendentals=0
        ),
    )(core, turns, in_hbm(activations), other, in_hbm(w_query), in_vmem(kv_rows))
    parts = lax.all_to_all(partial, "wide", 0, 0, tiled=True)
    attended = pl.pallas_call(
        attend_kernel,
        out_shape=jax.ShapeDtypeStruct((receivers, heads, HD), BF16),
        in_specs=[SMEM, VMEM, VMEM, VMEM, VMEM],
        out_specs=VMEM,
        compiler_params=pltpu.CompilerParams(vmem_limit_bytes=8 * MIB),
        cost_estimate=pl.CostEstimate(
            flops=SPAN, bytes_accessed=2 * MIB, transcendentals=heads * 2048
        ),
    )(lengths, turns, parts, cache_keys[0], cache_values[0])
    gathered = lax.all_to_all(attended, "wide", 0, 0, tiled=True)
    keep, send = pl.pallas_call(
        output_kernel,
        out_shape=[jax.ShapeDtypeStruct((rows // 2, out_cols), F32)] * 2,
        in_specs=[SMEM, VMEM, VMEM],
        out_specs=[VMEM, VMEM],
        compiler_params=pltpu.CompilerParams(vmem_limit_bytes=20 * MIB),
        cost_estimate=pl.CostEstimate(
            flops=2 * rows * heads * HD * out_cols, bytes_accessed=16 * MIB, transcendentals=0
        ),
    )(core, gathered.reshape(rows * heads, HD), in_vmem(w_out))
    return (keep + lax.ppermute(send, "narrow", swap)).astype(BF16)


def solution(mesh):
    placed = (
        P(("grp", "narrow"), "wide"),
        P("wide", "narrow"),
        P("wide", "narrow", None, None),
        P(("grp", "wide"), "narrow", None, None),
        P(("grp", "wide"), "narrow", None, None),
        P(("grp", "wide")),
        P("narrow", "wide"),
    )
    return jax.shard_map(
        local, mesh=mesh, in_specs=placed, out_specs=P(("grp", "narrow"), "wide"), check_vma=False
    )
```

```python
import functools
import math

import jax
import jax.numpy as jnp
from jax import lax
from jax.experimental import pallas as pl
from jax.experimental.pallas import tpu as pltpu
from jax.sharding import PartitionSpec as P

HD = 128
SUB = 4
ROPE_BASE = 500000.0
MIB = 2**20
F32, BF16 = jnp.float32, jnp.bfloat16
SPAN = 7_000_000_000
VMEM = pl.BlockSpec(memory_space=pltpu.VMEM)
SMEM = pl.BlockSpec(memory_space=pltpu.SMEM)
ANY = pl.BlockSpec(memory_space=pl.ANY)


def in_hbm(array):
    return pltpu.with_memory_space_constraint(array, pltpu.HBM)


def in_vmem(array):
    return pltpu.with_memory_space_constraint(array, pltpu.VMEM)


def turns_kernel(cosine_ref, sine_ref, out_ref):
    cosine, sine = cosine_ref[...], sine_ref[...]
    out_ref[...] = jnp.concatenate(
        [jnp.concatenate([cosine, cosine], axis=1), jnp.concatenate([-sine, sine], axis=1)], axis=0
    )


def project_kernel(
    heights, core_ref, after_ref, own_hbm, other_ref, w_ref, kv_ref, sums, own_ref, w, held, sems
):
    depth, cols = w_ref.shape
    own_copy = pltpu.make_async_copy(own_hbm, own_ref, sems.at[len(heights)])
    own_copy.start()
    copies, spans, at = [], [], 0
    for c, height in enumerate(heights):
        span = pl.ds(at, height)
        copies.append(pltpu.make_async_copy(w_ref.at[span], w.at[span], sems.at[c]))
        copies[-1].start()
        spans.append((at, height))
        at += height

    own_copy.wait()
    own, other = own_ref[...].astype(F32), other_ref[...].astype(F32)
    first = core_ref[0] == 0
    wide_rows = jnp.where(
        first, jnp.concatenate([own, other], axis=0), jnp.concatenate([other, own], axis=0)
    )
    rows = wide_rows.astype(BF16)
    count = rows.shape[0]
    heads = cols // HD

    parts = kv_ref.shape[0] // depth
    tiles = depth // HD
    stacked = jnp.concatenate(
        [wide_rows[:, t * HD : (t + 1) * HD] for t in range(tiles)], axis=0
    ).astype(BF16)
    spread_of = lax.broadcasted_iota(jnp.int32, (HD, parts * HD), 0)
    spread_to = lax.broadcasted_iota(jnp.int32, (HD, parts * HD), 1)
    spread = jnp.where(spread_to // parts == spread_of, 1.0, 0.0).astype(BF16)
    repeated = jnp.dot(stacked, spread, preferred_element_type=F32)
    slot = lax.broadcasted_iota(jnp.int32, (count, parts * HD), 1) % parts
    total = None
    for t in range(tiles):
        block = repeated[t * count : (t + 1) * count]
        left = jnp.concatenate(
            [jnp.where(slot == p, block, 0.0) for p in range(parts)], axis=0
        ).astype(BF16)
        part = jnp.dot(
            left, kv_ref[t * parts * HD : (t + 1) * parts * HD, :], preferred_element_type=F32
        )
        total = part if total is None else total + part
    for p in range(parts):
        sums[:, (heads + p) // SUB, (heads + p) % SUB, :] = total[p * count : (p + 1) * count]

    for c, (at, height) in enumerate(spans):
        copies[c].wait()
        block = jnp.dot(
            rows[:, at : at + height], w[at : at + height, :], preferred_element_type=F32
        )
        if c > 0:
            block = block + held[...]
        if c < len(spans) - 1:
            held[...] = block
    for h in range(heads):
        sums[:, h // SUB, h % SUB, :] = block[:, h * HD : (h + 1) * HD]


def attend_kernel(length_ref, turns_ref, parts_ref, keys_ref, values_ref, out_ref):
    summed = parts_ref[0]
    for i in range(1, parts_ref.shape[0]):
        summed = summed + parts_ref[i]
    summed = jnp.concatenate([summed[i] for i in range(summed.shape[0])], axis=0)
    kv_heads = keys_ref.shape[0]
    heads = summed.shape[0] - 2 * kv_heads
    group = heads // kv_heads
    slots = keys_ref.shape[1]
    rotated = summed * turns_ref[:1] + pltpu.roll(summed, HD // 2, 1) * turns_ref[1:]
    rotated = rotated.astype(BF16)
    scale = 1.0 / math.sqrt(HD)
    length = length_ref[0]
    visible = lax.broadcasted_iota(jnp.int32, (heads, slots), 1) < length
    groups = [slice(k * group, (k + 1) * group) for k in range(kv_heads)]
    scores = [
        lax.dot_general(
            rotated[rows], keys_ref[k], (((1,), (1,)), ((), ())), preferred_element_type=F32
        )
        for k, rows in enumerate(groups)
    ]
    scores = jnp.concatenate(scores, axis=0) * scale
    new_key, new_value = [], []
    for k in range(kv_heads):
        at = heads + 2 * k
        new_key.append(jnp.broadcast_to(rotated[at : at + 1].astype(F32), (group, HD)))
        value = summed[at + 1 : at + 2].astype(BF16).astype(F32)
        new_value.append(jnp.broadcast_to(value, (group, HD)))
    new_key, new_value = jnp.concatenate(new_key, axis=0), jnp.concatenate(new_value, axis=0)
    own = jnp.sum(rotated[:heads].astype(F32) * new_key, axis=-1, keepdims=True) * scale
    scores = jnp.where(visible, scores, -1e30)
    top = jnp.maximum(jnp.max(scores, axis=-1, keepdims=True), own)
    weights = jnp.where(visible, jnp.exp(scores - top), 0.0)
    own_weight = jnp.exp(own - top)
    inverse = 1.0 / (jnp.sum(weights, axis=-1, keepdims=True) + own_weight)
    probabilities = (weights * inverse).astype(BF16)
    own_prob = (own_weight * inverse).astype(BF16).astype(F32)
    result = [
        jnp.dot(probabilities[rows], values_ref[k], preferred_element_type=F32)
        for k, rows in enumerate(groups)
    ]
    block = (jnp.concatenate(result, axis=0) + own_prob * new_value).astype(BF16)
    for i in range(out_ref.shape[0]):
        out_ref[i] = block


def output_kernel(core_ref, flat_ref, w_ref, keep_ref, send_ref):
    depth, cols = w_ref.shape
    count = keep_ref.shape[0] * 2
    heads = depth // HD
    size = 8 * heads
    to = lax.broadcasted_iota(jnp.int32, (size, size), 0)
    come = lax.broadcasted_iota(jnp.int32, (size, size), 1)
    order = jnp.where((to % 8) * heads + to // 8 == come, 1.0, 0.0).astype(BF16)
    groups = [
        jnp.dot(order, flat_ref[g * size : (g + 1) * size, :], preferred_element_type=F32)
        for g in range(count // 8)
    ]
    left = jnp.concatenate(
        [
            jnp.concatenate([part[h * 8 : (h + 1) * 8] for part in groups], axis=0)
            for h in range(heads)
        ],
        axis=1,
    ).astype(BF16)
    half = count // 2
    first = core_ref[0] == 0
    width = 1024
    for c in range(cols // width):
        span = slice(c * width, (c + 1) * width)
        part = jnp.dot(left, w_ref[:, span], preferred_element_type=F32)
        low, high = part[:half, :], part[half:, :]
        keep_ref[:, span] = jnp.where(first, low, high)
        send_ref[:, span] = jnp.where(first, high, low)


def local(activations, w_query, w_keyval, cache_keys, cache_values, lengths, w_out):
    receivers = lax.axis_size("wide")
    core = lax.axis_index("narrow").astype(jnp.int32).reshape(1)
    swap = [(0, 1), (1, 0)]
    rows = activations.shape[0] * 2
    depth, cols = w_query.shape
    kv_heads = w_keyval.shape[1]
    heads = cols // HD
    out_cols = w_out.shape[1]
    half_width = HD // 2

    frequency = ROPE_BASE ** (-jnp.arange(half_width, dtype=F32) / half_width)
    angles = lengths.astype(F32)[:, None] * frequency[None, :]
    cosine, sine = jnp.cos(angles), jnp.sin(angles)
    turns = pl.pallas_call(
        turns_kernel,
        out_shape=jax.ShapeDtypeStruct((2, HD), F32),
        in_specs=[VMEM, VMEM],
        out_specs=VMEM,
        compiler_params=pltpu.CompilerParams(vmem_limit_bytes=MIB),
        cost_estimate=pl.CostEstimate(flops=SPAN, bytes_accessed=MIB, transcendentals=0),
    )(cosine, sine)

    other = lax.ppermute(activations, "narrow", swap)
    heights = [depth // 8] * 7 + [depth // 16] + [depth // 32] * 2 if depth % 512 == 0 else [depth]
    kv_rows = w_keyval.reshape(depth * kv_heads * 2, HD)
    partial = pl.pallas_call(
        functools.partial(project_kernel, heights),
        out_shape=pltpu.VMEM((rows, (heads + 2 * kv_heads) // SUB, SUB, HD), F32),
        in_specs=[SMEM, ANY, ANY, VMEM, ANY, VMEM],
        out_specs=VMEM,
        scratch_shapes=[
            pltpu.VMEM(activations.shape, BF16),
            pltpu.VMEM((depth, cols), BF16),
            pltpu.VMEM((rows, cols), F32),
            pltpu.SemaphoreType.DMA((len(heights) + 1,)),
        ],
        compiler_params=pltpu.CompilerParams(vmem_limit_bytes=24 * MIB),
        cost_estimate=pl.CostEstimate(
            flops=SPAN, bytes_accessed=18 * MIB, transcendentals=0
        ),
    )(core, turns, in_hbm(activations), other, in_hbm(w_query), in_vmem(kv_rows))
    parts = lax.all_to_all(partial, "wide", 0, 0, tiled=True)
    attended = pl.pallas_call(
        attend_kernel,
        out_shape=jax.ShapeDtypeStruct((receivers, heads, HD), BF16),
        in_specs=[SMEM, VMEM, VMEM, VMEM, VMEM],
        out_specs=VMEM,
        compiler_params=pltpu.CompilerParams(vmem_limit_bytes=8 * MIB),
        cost_estimate=pl.CostEstimate(
            flops=SPAN, bytes_accessed=2 * MIB, transcendentals=heads * 2048
        ),
    )(lengths, turns, parts, cache_keys[0], cache_values[0])
    gathered = lax.all_to_all(attended, "wide", 0, 0, tiled=True)
    keep, send = pl.pallas_call(
        output_kernel,
        out_shape=[jax.ShapeDtypeStruct((rows // 2, out_cols), F32)] * 2,
        in_specs=[SMEM, VMEM, VMEM],
        out_specs=[VMEM, VMEM],
        compiler_params=pltpu.CompilerParams(vmem_limit_bytes=20 * MIB),
        cost_estimate=pl.CostEstimate(
            flops=2 * rows * heads * HD * out_cols, bytes_accessed=16 * MIB, transcendentals=0
        ),
    )(core, gathered.reshape(rows * heads, HD), in_vmem(w_out))
    return (keep + lax.ppermute(send, "narrow", swap)).astype(BF16)


def solution(mesh):
    placed = (
        P(("grp", "narrow"), "wide"),
        P("wide", "narrow"),
        P("wide", "narrow", None, None),
        P(("grp", "wide"), "narrow", None, None),
        P(("grp", "wide"), "narrow", None, None),
        P(("grp", "wide")),
        P("narrow", "wide"),
    )
    return jax.shard_map(
        local, mesh=mesh, in_specs=placed, out_specs=P(("grp", "narrow"), "wide"), check_vma=False
    )
```

```python
import functools
import math

import jax
import jax.numpy as jnp
from jax import lax
from jax.experimental import pallas as pl
from jax.experimental.pallas import tpu as pltpu
from jax.sharding import PartitionSpec as P

HD = 128
SUB = 4
ROPE_BASE = 500000.0
MIB = 2**20
F32, BF16 = jnp.float32, jnp.bfloat16
SPAN = 7_000_000_000
VMEM = pl.BlockSpec(memory_space=pltpu.VMEM)
SMEM = pl.BlockSpec(memory_space=pltpu.SMEM)
ANY = pl.BlockSpec(memory_space=pl.ANY)


def in_hbm(array):
    return pltpu.with_memory_space_constraint(array, pltpu.HBM)


def in_vmem(array):
    return pltpu.with_memory_space_constraint(array, pltpu.VMEM)


def turns_kernel(cosine_ref, sine_ref, out_ref):
    cosine, sine = cosine_ref[...], sine_ref[...]
    out_ref[...] = jnp.concatenate(
        [jnp.concatenate([cosine, cosine], axis=1), jnp.concatenate([-sine, sine], axis=1)], axis=0
    )


def project_kernel(
    heights, core_ref, after_ref, own_hbm, other_ref, w_ref, kv_ref, sums, own_ref, w, held, sems
):
    depth, cols = w_ref.shape
    own_copy = pltpu.make_async_copy(own_hbm, own_ref, sems.at[len(heights)])
    own_copy.start()
    copies, spans, at = [], [], 0
    for c, height in enumerate(heights):
        span = pl.ds(at, height)
        copies.append(pltpu.make_async_copy(w_ref.at[span], w.at[span], sems.at[c]))
        copies[-1].start()
        spans.append((at, height))
        at += height

    own_copy.wait()
    own, other = own_ref[...].astype(F32), other_ref[...].astype(F32)
    first = core_ref[0] == 0
    wide_rows = jnp.where(
        first, jnp.concatenate([own, other], axis=0), jnp.concatenate([other, own], axis=0)
    )
    rows = wide_rows.astype(BF16)
    count = rows.shape[0]
    heads = cols // HD

    parts = kv_ref.shape[0] // depth
    tiles = depth // HD
    stacked = jnp.concatenate(
        [wide_rows[:, t * HD : (t + 1) * HD] for t in range(tiles)], axis=0
    ).astype(BF16)
    spread_of = lax.broadcasted_iota(jnp.int32, (HD, parts * HD), 0)
    spread_to = lax.broadcasted_iota(jnp.int32, (HD, parts * HD), 1)
    spread = jnp.where(spread_to // parts == spread_of, 1.0, 0.0).astype(BF16)
    repeated = jnp.dot(stacked, spread, preferred_element_type=F32)
    slot = lax.broadcasted_iota(jnp.int32, (count, parts * HD), 1) % parts
    for c, (at, height) in enumerate(spans):
        copies[c].wait()
        block = jnp.dot(
            rows[:, at : at + height], w[at : at + height, :], preferred_element_type=F32
        )
        if c > 0:
            block = block + held[...]
        if c < len(spans) - 1:
            held[...] = block
        if c == min(1, len(spans) - 1):
            total = None
            for t in range(tiles):
                piece = repeated[t * count : (t + 1) * count]
                left = jnp.concatenate(
                    [jnp.where(slot == p, piece, 0.0) for p in range(parts)], axis=0
                ).astype(BF16)
                part = jnp.dot(
                    left, kv_ref[t * parts * HD : (t + 1) * parts * HD, :], preferred_element_type=F32
                )
                total = part if total is None else total + part
            for p in range(parts):
                sums[:, (heads + p) // SUB, (heads + p) % SUB, :] = total[p * count : (p + 1) * count]
    for h in range(heads):
        sums[:, h // SUB, h % SUB, :] = block[:, h * HD : (h + 1) * HD]


def attend_kernel(length_ref, turns_ref, parts_ref, keys_ref, values_ref, out_ref):
    summed = parts_ref[0]
    for i in range(1, parts_ref.shape[0]):
        summed = summed + parts_ref[i]
    summed = jnp.concatenate([summed[i] for i in range(summed.shape[0])], axis=0)
    kv_heads = keys_ref.shape[0]
    heads = summed.shape[0] - 2 * kv_heads
    group = heads // kv_heads
    slots = keys_ref.shape[1]
    rotated = summed * turns_ref[:1] + pltpu.roll(summed, HD // 2, 1) * turns_ref[1:]
    rotated = rotated.astype(BF16)
    scale = 1.0 / math.sqrt(HD)
    length = length_ref[0]
    visible = lax.broadcasted_iota(jnp.int32, (heads, slots), 1) < length
    groups = [slice(k * group, (k + 1) * group) for k in range(kv_heads)]
    scores = [
        lax.dot_general(
            rotated[rows], keys_ref[k], (((1,), (1,)), ((), ())), preferred_element_type=F32
        )
        for k, rows in enumerate(groups)
    ]
    scores = jnp.concatenate(scores, axis=0) * scale
    new_key, new_value = [], []
    for k in range(kv_heads):
        at = heads + 2 * k
        new_key.append(jnp.broadcast_to(rotated[at : at + 1].astype(F32), (group, HD)))
        value = summed[at + 1 : at + 2].astype(BF16).astype(F32)
        new_value.append(jnp.broadcast_to(value, (group, HD)))
    new_key, new_value = jnp.concatenate(new_key, axis=0), jnp.concatenate(new_value, axis=0)
    own = jnp.sum(rotated[:heads].astype(F32) * new_key, axis=-1, keepdims=True) * scale
    scores = jnp.where(visible, scores, -1e30)
    top = jnp.maximum(jnp.max(scores, axis=-1, keepdims=True), own)
    weights = jnp.where(visible, jnp.exp(scores - top), 0.0)
    own_weight = jnp.exp(own - top)
    inverse = 1.0 / (jnp.sum(weights, axis=-1, keepdims=True) + own_weight)
    probabilities = (weights * inverse).astype(BF16)
    own_prob = (own_weight * inverse).astype(BF16).astype(F32)
    result = [
        jnp.dot(probabilities[rows], values_ref[k], preferred_element_type=F32)
        for k, rows in enumerate(groups)
    ]
    block = (jnp.concatenate(result, axis=0) + own_prob * new_value).astype(BF16)
    for i in range(out_ref.shape[0]):
        out_ref[i] = block


def output_kernel(core_ref, flat_ref, w_ref, keep_ref, send_ref):
    depth, cols = w_ref.shape
    count = keep_ref.shape[0] * 2
    heads = depth // HD
    size = 8 * heads
    to = lax.broadcasted_iota(jnp.int32, (size, size), 0)
    come = lax.broadcasted_iota(jnp.int32, (size, size), 1)
    order = jnp.where((to % 8) * heads + to // 8 == come, 1.0, 0.0).astype(BF16)
    groups = [
        jnp.dot(order, flat_ref[g * size : (g + 1) * size, :], preferred_element_type=F32)
        for g in range(count // 8)
    ]
    left = jnp.concatenate(
        [
            jnp.concatenate([part[h * 8 : (h + 1) * 8] for part in groups], axis=0)
            for h in range(heads)
        ],
        axis=1,
    ).astype(BF16)
    half = count // 2
    first = core_ref[0] == 0
    width = 1024
    for c in range(cols // width):
        span = slice(c * width, (c + 1) * width)
        part = jnp.dot(left, w_ref[:, span], preferred_element_type=F32)
        low, high = part[:half, :], part[half:, :]
        keep_ref[:, span] = jnp.where(first, low, high)
        send_ref[:, span] = jnp.where(first, high, low)


def local(activations, w_query, w_keyval, cache_keys, cache_values, lengths, w_out):
    receivers = lax.axis_size("wide")
    core = lax.axis_index("narrow").astype(jnp.int32).reshape(1)
    swap = [(0, 1), (1, 0)]
    rows = activations.shape[0] * 2
    depth, cols = w_query.shape
    kv_heads = w_keyval.shape[1]
    heads = cols // HD
    out_cols = w_out.shape[1]
    half_width = HD // 2

    frequency = ROPE_BASE ** (-jnp.arange(half_width, dtype=F32) / half_width)
    angles = lengths.astype(F32)[:, None] * frequency[None, :]
    cosine, sine = jnp.cos(angles), jnp.sin(angles)
    turns = pl.pallas_call(
        turns_kernel,
        out_shape=jax.ShapeDtypeStruct((2, HD), F32),
        in_specs=[VMEM, VMEM],
        out_specs=VMEM,
        compiler_params=pltpu.CompilerParams(vmem_limit_bytes=MIB),
        cost_estimate=pl.CostEstimate(flops=SPAN, bytes_accessed=MIB, transcendentals=0),
    )(cosine, sine)

    other = lax.ppermute(activations, "narrow", swap)
    heights = [depth // 8] * 7 + [depth // 16] + [depth // 32] * 2 if depth % 512 == 0 else [depth]
    kv_rows = w_keyval.reshape(depth * kv_heads * 2, HD)
    partial = pl.pallas_call(
        functools.partial(project_kernel, heights),
        out_shape=pltpu.VMEM((rows, (heads + 2 * kv_heads) // SUB, SUB, HD), F32),
        in_specs=[SMEM, ANY, ANY, VMEM, ANY, VMEM],
        out_specs=VMEM,
        scratch_shapes=[
            pltpu.VMEM(activations.shape, BF16),
            pltpu.VMEM((depth, cols), BF16),
            pltpu.VMEM((rows, cols), F32),
            pltpu.SemaphoreType.DMA((len(heights) + 1,)),
        ],
        compiler_params=pltpu.CompilerParams(vmem_limit_bytes=24 * MIB),
        cost_estimate=pl.CostEstimate(
            flops=SPAN, bytes_accessed=18 * MIB, transcendentals=0
        ),
    )(core, turns, in_hbm(activations), other, in_hbm(w_query), in_vmem(kv_rows))
    parts = lax.all_to_all(partial, "wide", 0, 0, tiled=True)
    attended = pl.pallas_call(
        attend_kernel,
        out_shape=jax.ShapeDtypeStruct((receivers, heads, HD), BF16),
        in_specs=[SMEM, VMEM, VMEM, VMEM, VMEM],
        out_specs=VMEM,
        compiler_params=pltpu.CompilerParams(vmem_limit_bytes=8 * MIB),
        cost_estimate=pl.CostEstimate(
            flops=SPAN, bytes_accessed=2 * MIB, transcendentals=heads * 2048
        ),
    )(lengths, turns, parts, cache_keys[0], cache_values[0])
    gathered = lax.all_to_all(attended, "wide", 0, 0, tiled=True)
    keep, send = pl.pallas_call(
        output_kernel,
        out_shape=[jax.ShapeDtypeStruct((rows // 2, out_cols), F32)] * 2,
        in_specs=[SMEM, VMEM, VMEM],
        out_specs=[VMEM, VMEM],
        compiler_params=pltpu.CompilerParams(vmem_limit_bytes=20 * MIB),
        cost_estimate=pl.CostEstimate(
            flops=2 * rows * heads * HD * out_cols, bytes_accessed=16 * MIB, transcendentals=0
        ),
    )(core, gathered.reshape(rows * heads, HD), in_vmem(w_out))
    return (keep + lax.ppermute(send, "narrow", swap)).astype(BF16)


def solution(mesh):
    placed = (
        P(("grp", "narrow"), "wide"),
        P("wide", "narrow"),
        P("wide", "narrow", None, None),
        P(("grp", "wide"), "narrow", None, None),
        P(("grp", "wide"), "narrow", None, None),
        P(("grp", "wide")),
        P("narrow", "wide"),
    )
    return jax.shard_map(
        local, mesh=mesh, in_specs=placed, out_specs=P(("grp", "narrow"), "wide"), check_vma=False
    )
```
